32 devices in a mesh: dp: 32 (over z, y, x, core).
Axes of the slice: x: 2, y: 2, z: 4, core: 2. Of those that a mesh axis runs over, the one named last changes fastest.
Arguments:
- tokens: bfloat16 [32768, 576], P('dp'), may hold values from -6 to 6
- segment_ids: int32 [32768], P('dp'), may hold values from -1 to 7, as said below
- cotangent: bfloat16 [32768, 576], P('dp'), may hold values from -6 to 6
- w_query: bfloat16 [331776], P('dp'), may hold values from -0.25 to 0.25
- w_key: bfloat16 [110592], P('dp'), may hold values from -0.25 to 0.25
- w_value: bfloat16 [110592], P('dp'), may hold values from -0.25 to 0.25
- w_output: bfloat16 [331776], P('dp'), may hold values from -1 to 1
- norm_gains: bfloat16 [1152], P('dp'), may hold values from 0.5 to 1.5
- w_gate: bfloat16 [884736], P('dp'), may hold values from -0.25 to 0.25
- w_up: bfloat16 [884736], P('dp'), may hold values from -0.25 to 0.25
- w_down: bfloat16 [884736], P('dp'), may hold values from -0.15625 to 0.15625
Outputs:
- layer_out: bfloat16 [32768, 576], P('dp')
- tokens_grad: bfloat16 [32768, 576], P('dp')
- grad_query: float32 [331776], P('dp')
- grad_key: float32 [110592], P('dp')
- grad_value: float32 [110592], P('dp')
- grad_output: float32 [331776], P('dp')
- grad_gains: float32 [1152], P('dp')
- grad_gate: float32 [884736], P('dp')
- grad_up: float32 [884736], P('dp')
- grad_down: float32 [884736], P('dp')
The draws below stay inside these ranges and needn't reach their ends.
Inputs may be any that keep to these rules, and one draw needn't show every extreme that they name: `segment_ids`: within each device's 1024 slots the live tokens come first, numbered by sequence from 0 upward in runs (one run a sequence, at most 8 sequences a device), and -1 marks the unused slots after them; every device holds 512 live tokens or more; some device holds a single sequence of all 1024 slots, and some device holds 8 sequences.
All inputs are finite; a program needn't handle non-finite values.
Results may differ from the reference program's by a relative error of at most 0.012.
Values may be sent and summed in bfloat16 or wider, within the bound.
A program may use at most 128 MiB of HBM per device.

```python
import jax
import jax.numpy as jnp
from jax import lax

D = 576
HEADS = 9
KV_HEADS = 3
HEAD_DIM = 64
FF = 1536
TOK_DEV = 1024
KVW = 192
TOKENS = 32768
GAINS = 1152


def draw_segment_ids(key, part):
    key = jax.random.fold_in(key, 7)
    key_count, key_full, key_cut = jax.random.split(key, 3)
    device_count = TOKENS // TOK_DEV
    live_rows = jax.random.randint(key_count, (device_count, 1), TOK_DEV // 2, TOK_DEV + 1)
    full_device = jax.random.randint(key_full, (), 0, device_count)
    many_device = (full_device + 1) % device_count
    device = jnp.arange(device_count, dtype=jnp.int32)[:, None]
    live_rows = jnp.where(device == full_device, TOK_DEV, live_rows)
    position = jnp.arange(TOK_DEV, dtype=jnp.int32)[None, :]
    stride = TOK_DEV // 16
    marks = (position % stride == 0) & (position < 8 * stride)
    new_sequence = jax.random.randint(key_cut, (device_count, TOK_DEV), 0, TOK_DEV) < 4
    new_sequence = new_sequence & (device != full_device) | (position == 0) | (device == many_device) & marks
    numbers = jnp.minimum(jnp.cumsum(new_sequence.astype(jnp.int32), axis=1) - 1, 7)
    return jnp.where(position < live_rows, numbers, -1).reshape(device_count * TOK_DEV).astype(jnp.int32)


def block_scale(own_key, shape, cuts, low, high):
    loudness = 1.0
    for dim, shards_of in cuts:
        heights = jax.random.uniform(jax.random.fold_in(jax.random.fold_in(own_key, 6), dim), (shards_of,), jnp.float32, low / len(cuts), high / len(cuts))
        loudness = loudness * jnp.repeat(jnp.exp(heights), shape[dim] // shards_of).reshape((-1,) + (1,) * (len(shape) - 1 - dim))
    return loudness


def bell_draw(stream_key, dims, deviation, reach, cuts=(), kind=jnp.bfloat16):
    entries = deviation * jax.random.normal(stream_key, dims, jnp.float32)
    if cuts:
        entries = entries * block_scale(stream_key, dims, cuts, -0.22, 0.18)
    return jnp.clip(entries, -reach, reach).astype(kind)


def setup_inputs(seed: int = 0) -> dict:
    key_of = jax.random.split(jax.random.key(seed), 12)
    tokens = bell_draw(key_of[0], (TOKENS, D), 1.0, 6.0, ((0, 32),))
    segment_ids = draw_segment_ids(jax.random.fold_in(key_of[11], 71), 0)
    cotangent = bell_draw(key_of[2], (TOKENS, D), 1.0, 6.0, ((0, 32),))
    w_query = bell_draw(key_of[3], (D * D,), D ** -0.5, 0.25, ((0, 32),))
    w_key = bell_draw(key_of[4], (D * KVW,), D ** -0.5, 0.25, ((0, 32),))
    w_value = bell_draw(key_of[5], (D * KVW,), D ** -0.5, 0.25, ((0, 32),))
    w_output = bell_draw(key_of[6], (D * D,), (D // 16) ** -0.5, 1.0, ((0, 32),))
    norm_gains = jnp.clip(1.0 + 0.1 * jax.random.normal(key_of[7], (GAINS,), jnp.float32), 0.5, 1.5).astype(jnp.bfloat16)
    w_gate = bell_draw(key_of[8], (D * FF,), D ** -0.5, 0.25, ((0, 32),))
    w_up = bell_draw(key_of[9], (D * FF,), D ** -0.5, 0.25, ((0, 32),))
    w_down = bell_draw(key_of[10], (FF * D,), FF ** -0.5, 0.15625, ((0, 32),))
    return {"tokens": tokens, "segment_ids": segment_ids, "cotangent": cotangent, "w_query": w_query, "w_key": w_key, "w_value": w_value, "w_output": w_output, "norm_gains": norm_gains, "w_gate": w_gate, "w_up": w_up, "w_down": w_down}


EPS = 1e-05
NEG = -1e+30
THETA = 100000.0

@jax.custom_vjp
def low(v):
    return lax.optimization_barrier(v.astype(jnp.bfloat16)).astype(jnp.float32)

@jax.custom_vjp
def low_back(v):
    return v

def low_keep(v):
    return (low(v), None)

def low_pass(kept, grad):
    return (grad,)

def back_keep(v):
    return (v, None)

def back_low(kept, grad):
    return (low(grad),)
low.defvjp(low_keep, low_pass)
low_back.defvjp(back_keep, back_low)

def rms_norm(stream, gain_vec):
    return stream * lax.rsqrt(lax.optimization_barrier(jnp.mean(stream * stream, axis=-1, keepdims=True)) + EPS) * gain_vec

def rope_tables(seg_ids):
    length_rows = seg_ids.shape[0]
    position = jnp.arange(length_rows, dtype=jnp.int32)
    starts = jnp.concatenate([jnp.ones((1,), dtype=jnp.bool_), seg_ids[1:] != seg_ids[:-1]])
    run_start = lax.cummax(jnp.where(starts, position, 0), axis=0)
    offsets = (position - run_start).astype(jnp.float32)
    inverse_freq = THETA ** (-jnp.arange(0, HEAD_DIM, 2, dtype=jnp.float32) / HEAD_DIM)
    angles = offsets[:, None] * inverse_freq[None, :]
    angles = jnp.concatenate([angles, angles], axis=-1)
    return (jnp.cos(angles), jnp.sin(angles))

def rotate(heads_in, cos_table, sin_table):
    half_width = heads_in.shape[-1] // 2
    turned = jnp.concatenate([-heads_in[..., half_width:], heads_in[..., :half_width]], axis=-1)
    return heads_in * cos_table[:, None, :] + turned * sin_table[:, None, :]

def allowed_keys(query_ids, key_ids, query_start):
    query_pos = query_start + jnp.arange(query_ids.shape[0], dtype=jnp.int32)
    key_pos = jnp.arange(key_ids.shape[0], dtype=jnp.int32)
    same_seq = (query_ids[:, None] == key_ids[None, :]) & (query_ids[:, None] >= 0)
    causal = query_pos[:, None] >= key_pos[None, :]
    return same_seq & causal | (query_pos[:, None] == key_pos[None, :])

def layer_block(stream, seg_ids, weight_query, weight_key, weight_value, weight_output, gain_one, gain_two, weight_gate, weight_up, weight_down):
    highest = lax.Precision.HIGHEST
    row_count = stream.shape[0]
    group_size = HEADS // KV_HEADS
    cos_table, sin_table = rope_tables(seg_ids)
    attn_input = low(rms_norm(stream, gain_one))
    query_pre = low_back(jnp.dot(attn_input, weight_query, precision=highest)).reshape(row_count, HEADS, HEAD_DIM)
    key_pre = low_back(jnp.dot(attn_input, weight_key, precision=highest)).reshape(row_count, KV_HEADS, HEAD_DIM)
    values = low(low_back(jnp.dot(attn_input, weight_value, precision=highest))).reshape(row_count, KV_HEADS, HEAD_DIM)
    query_rot = low(rotate(query_pre, cos_table, sin_table)).reshape(row_count, KV_HEADS, group_size, HEAD_DIM)
    key_rot = low(rotate(key_pre, cos_table, sin_table))
    allowed = allowed_keys(seg_ids, seg_ids, 0)
    scores = low_back(jnp.einsum('qjgd,kjd->jgqk', query_rot, key_rot, precision=highest) * HEAD_DIM ** (-0.5))
    scores = jnp.where(allowed[None, None], scores, NEG)
    probability = low(jax.nn.softmax(scores, axis=-1))
    mixture = jnp.einsum('jgqk,kjd->qjgd', probability, values, precision=highest)
    mixture = low_back(low(mixture)).reshape(row_count, HEADS * HEAD_DIM)
    stream_mid = stream + low_back(jnp.dot(mixture, weight_output, precision=highest))
    mlp_input = low(rms_norm(stream_mid, gain_two))
    gate = low_back(jnp.dot(mlp_input, weight_gate, precision=highest))
    up_proj = low_back(jnp.dot(mlp_input, weight_up, precision=highest))
    activation = low(jax.nn.silu(gate) * up_proj)
    return stream_mid + low_back(jnp.dot(activation, weight_down, precision=highest))

def reference(tokens, segment_ids, cotangent, w_query, w_key, w_value, w_output, norm_gains, w_gate, w_up, w_down):
    device_count = TOKENS // TOK_DEV
    kv_width = KV_HEADS * HEAD_DIM
    seg_blocks = segment_ids.reshape(device_count, TOK_DEV)
    stream_in = tokens.astype(jnp.float32).reshape(device_count, TOK_DEV, D)

    def forward(stream_all, flat_query, flat_key, flat_value, flat_output, gains, flat_gate, flat_up, flat_down):
        weight_query = flat_query.reshape(D, D)
        weight_key = flat_key.reshape(D, kv_width)
        weight_value = flat_value.reshape(D, kv_width)
        weight_output = flat_output.reshape(D, D)
        gain_one = gains[:D]
        gain_two = gains[D:2 * D]
        weight_gate = flat_gate.reshape(D, FF)
        weight_up = flat_up.reshape(D, FF)
        weight_down = flat_down.reshape(FF, D)

        def one_block(pieces):
            return layer_block(pieces[0], pieces[1], weight_query, weight_key, weight_value, weight_output, gain_one, gain_two, weight_gate, weight_up, weight_down)
        return lax.map(jax.checkpoint(one_block), (stream_all, seg_blocks))
    layer_all, pullback = jax.vjp(forward, stream_in, w_query.astype(jnp.float32), w_key.astype(jnp.float32), w_value.astype(jnp.float32), w_output.astype(jnp.float32), norm_gains.astype(jnp.float32), w_gate.astype(jnp.float32), w_up.astype(jnp.float32), w_down.astype(jnp.float32))
    grads = pullback(cotangent.astype(jnp.float32).reshape(device_count, TOK_DEV, D))
    return (layer_all.reshape(TOKENS, D).astype(jnp.bfloat16), grads[0].reshape(TOKENS, D).astype(jnp.bfloat16), grads[1], grads[2], grads[3], grads[4], grads[5], grads[6], grads[7], grads[8])
```

```python
import functools

import jax
import jax.numpy as jnp
from jax import lax
from jax.experimental import pallas as pl
from jax.experimental.pallas import tpu as pltpu
from jax.sharding import PartitionSpec as P

D = 576
HEADS = 9
KV_HEADS = 3
HEAD_DIM = 64
FF = 1536
GROUP = HEADS // KV_HEADS
LANES = 128
VMEM_LIMIT = 56 * 1024 * 1024


EPS = 1e-05
THETA = 100000.0


def rms_norm(stream, gain_vec):
    return stream * lax.rsqrt(jnp.mean(stream * stream, axis=-1, keepdims=True) + EPS) * gain_vec


def rope_tables(seg_ids):
    length_rows = seg_ids.shape[0]
    position = jnp.arange(length_rows, dtype=jnp.int32)
    starts = jnp.concatenate([jnp.ones((1,), dtype=jnp.bool_), seg_ids[1:] != seg_ids[:-1]])
    before = position[:, None] >= position[None, :]
    run_start = jnp.max(jnp.where(before & starts[None, :], position[None, :], 0), axis=1)
    offsets = (position - run_start).astype(jnp.float32)
    inverse_freq = THETA ** (-jnp.arange(0, HEAD_DIM, 2, dtype=jnp.float32) / HEAD_DIM)
    angles = offsets[:, None] * inverse_freq[None, :]
    angles = jnp.concatenate([angles, angles], axis=-1)
    return (jnp.cos(angles), jnp.sin(angles))


def weight_grad(left_rows, right_rows):
    return lax.dot_general(
        left_rows, right_rows, (((0,), (0,)), ((), ())), preferred_element_type=jnp.float32
    )


def input_grad(grad_rows, weight):
    return lax.dot_general(
        grad_rows, weight, (((1,), (1,)), ((), ())), preferred_element_type=jnp.float32
    )


def bit_orders(bit_count):
    first = list(range(bit_count))
    second = list(first)
    if bit_count >= 3:
        second[-3], second[-2] = second[-2], second[-3]
    return (first, second)


def row_parts(rows):
    half = rows // 32 * 16
    return ((0, half), (half, rows - half)) if half else ((0, rows),)


def my_bits(bit_count):
    me = lax.axis_index("dp")
    bits = [lax.rem(lax.div(me, 2 ** (bit_count - 1 - b)), 2) for b in range(bit_count)]
    partners = [me + (1 - 2 * bits[b]) * 2 ** (bit_count - 1 - b) for b in range(bit_count)]
    return (bits, partners)


def greet(partners):
    barrier = pltpu.get_barrier_semaphore()
    for partner in partners:
        pl.semaphore_signal(
            barrier, inc=1, device_id=(partner,), device_id_type=pl.DeviceIdType.MESH
        )
    pl.semaphore_wait(barrier, len(partners))


def gather_kernel(bit_count, parts, packet_ref, out_ref, send_sem, recv_sem):
    bits, partners = my_bits(bit_count)
    greet(partners)
    out_ref[tuple(bits)] = packet_ref[...]
    orders = bit_orders(bit_count)

    def make(part, phase):
        order = orders[part]
        row_start, row_count = parts[part]
        at = tuple(slice(None) if b in order[:phase] else bits[b] for b in range(bit_count))
        at = at + (pl.ds(row_start, row_count),)
        return pltpu.make_async_remote_copy(
            src_ref=out_ref.at[at],
            dst_ref=out_ref.at[at],
            send_sem=send_sem.at[part, phase],
            recv_sem=recv_sem.at[part, phase],
            device_id=(partners[order[phase]],),
            device_id_type=pl.DeviceIdType.MESH,
        )

    copies = []
    for part in range(len(parts)):
        copies.append(make(part, 0))
        copies[part].start()
    for phase in range(bit_count):
        for part in range(len(parts)):
            copies[part].wait()
            if phase + 1 < bit_count:
                copies[part] = make(part, phase + 1)
                copies[part].start()


def gather_packets(packet, device_count, collective_id):
    bit_count = device_count.bit_length() - 1
    parts = row_parts(packet.shape[0])
    return pl.pallas_call(
        functools.partial(gather_kernel, bit_count, parts),
        out_shape=jax.ShapeDtypeStruct((2,) * bit_count + packet.shape, packet.dtype),
        in_specs=[pl.BlockSpec(memory_space=pltpu.VMEM)],
        out_specs=pl.BlockSpec(memory_space=pltpu.VMEM),
        scratch_shapes=[
            pltpu.SemaphoreType.DMA((2, bit_count)),
            pltpu.SemaphoreType.DMA((2, bit_count)),
        ],
        compiler_params=pltpu.CompilerParams(
            collective_id=collective_id, has_side_effects=True, vmem_limit_bytes=VMEM_LIMIT
        ),
    )(packet)


def scatter_kernel(bit_count, parts, grads_ref, out_ref, acc, *rest):
    arrived = rest[:bit_count]
    send_sem, recv_sem = rest[bit_count:]
    bits, partners = my_bits(bit_count)
    greet(partners)
    orders = [order[::-1] for order in bit_orders(bit_count)]
    last = bit_count - 1

    def make(part, phase):
        order = orders[part]
        row_start, row_count = parts[part]
        rows = pl.ds(row_start, row_count)
        bit = order[phase]
        at = tuple(
            bits[b] if b in order[:phase] else (1 - bits[b] if b == bit else slice(None))
            for b in range(bit_count)
        )
        source = grads_ref if phase == 0 else acc
        at = at if phase == 0 else at[:last]
        landing = (slice(None),) * (bit_count - 1 - phase) + (rows,)
        return pltpu.make_async_remote_copy(
            src_ref=source.at[at + (rows,)],
            dst_ref=arrived[phase].at[landing],
            send_sem=send_sem.at[part, phase],
            recv_sem=recv_sem.at[part, phase],
            device_id=(partners[bit],),
            device_id_type=pl.DeviceIdType.MESH,
        )

    def add(part, phase):
        order = orders[part]
        row_start, row_count = parts[part]
        rows = pl.ds(row_start, row_count)
        open_bits = [b for b in range(bit_count) if b not in order[: phase + 1]]

        def one(step, carry):
            digits = [
                lax.rem(lax.div(step, 2 ** (len(open_bits) - 1 - d)), 2)
                for d in range(len(open_bits))
            ]
            chosen = dict(zip(open_bits, digits))
            at = tuple(chosen.get(b, bits[b]) for b in range(bit_count))
            own = grads_ref[at + (rows,)] if phase == 0 else acc[at[:last] + (rows,)]
            total = own.astype(jnp.float32) + arrived[phase][tuple(digits) + (rows,)].astype(
                jnp.float32
            )
            if phase == last:
                out_ref[rows] = total
            else:
                acc[at[:last] + (rows,)] = total.astype(acc.dtype)
            return carry

        if open_bits:
            lax.fori_loop(0, 2 ** len(open_bits), one, 0)
        else:
            one(0, 0)

    copies = []
    for part in range(len(parts)):
        copies.append(make(part, 0))
        copies[part].start()
    for phase in range(bit_count):
        for part in range(len(parts)):
            copies[part].wait()
            add(part, phase)
            if phase + 1 < bit_count:
                copies[part] = make(part, phase + 1)
                copies[part].start()


def scatter_sums(grads, collective_id):
    bit_count = grads.ndim - 2
    packet_shape = grads.shape[-2:]
    parts = row_parts(packet_shape[0])
    return pl.pallas_call(
        functools.partial(scatter_kernel, bit_count, parts),
        out_shape=jax.ShapeDtypeStruct(packet_shape, jnp.float32),
        in_specs=[pl.BlockSpec(memory_space=pltpu.VMEM)],
        out_specs=pl.BlockSpec(memory_space=pltpu.VMEM),
        scratch_shapes=[pltpu.VMEM((2,) * (bit_count - 1) + packet_shape, grads.dtype)]
        + [
            pltpu.VMEM((2,) * (bit_count - 1 - phase) + packet_shape, grads.dtype)
            for phase in range(bit_count)
        ]
        + [
            pltpu.SemaphoreType.DMA((2, bit_count)),
            pltpu.SemaphoreType.DMA((2, bit_count)),
        ],
        compiler_params=pltpu.CompilerParams(
            collective_id=collective_id, has_side_effects=True, vmem_limit_bytes=VMEM_LIMIT
        ),
    )(grads)


def masked_scores(query_ids, key_ids, queries, keys, start, finish, block_rows):
    raw = lax.dot_general(
        queries, keys, (((1,), (1,)), ((), ())), preferred_element_type=jnp.float32
    ) * HEAD_DIM ** (-0.5)
    row_at = start + lax.broadcasted_iota(jnp.int32, (block_rows, finish), 0)
    col_at = lax.broadcasted_iota(jnp.int32, (block_rows, finish), 1)
    allowed = (query_ids == key_ids) & (row_at >= col_at)
    bias = jnp.where(allowed, 0.0, -1e30)
    return raw.reshape(GROUP, block_rows, finish) + bias[None]


def attend_kernel(block_rows, query_ids, key_ids, q_ref, k_ref, v_ref, o_ref, lse_ref):
    row_count = q_ref.shape[1]
    for start in range(0, row_count, block_rows):
        finish = start + block_rows
        rows = slice(start, finish)
        queries = q_ref[:, rows].reshape(GROUP * block_rows, HEAD_DIM)
        scores = masked_scores(
            query_ids[rows], key_ids[:, :finish], queries, k_ref[0, :finish], start, finish, block_rows
        ).reshape(GROUP * block_rows, finish)
        peak = jnp.max(scores, axis=-1, keepdims=True)
        expos = jnp.exp(scores - peak)
        exp_total = jnp.sum(expos, axis=-1, keepdims=True)
        probability = (expos * (1.0 / exp_total)).astype(jnp.bfloat16)
        mixed = jnp.dot(probability, v_ref[0, :finish], preferred_element_type=jnp.float32)
        o_ref[:, rows] = mixed.astype(jnp.bfloat16).reshape(GROUP, block_rows, HEAD_DIM)
        lse_ref[:, rows] = (peak + jnp.log(exp_total)).reshape(GROUP, block_rows, 1)


def turn_back(grad, cos_table, sin_table):
    half = HEAD_DIM // 2
    by_sin = grad * sin_table
    return grad * cos_table + jnp.concatenate([by_sin[:, half:], -by_sin[:, :half]], axis=-1)


def attend_back_kernel(
    block_rows, query_ids, key_ids, cos_ref, sin_ref, q_ref, k_ref, v_ref, do_ref, lse_ref,
    dq_ref, dk_ref, dv_ref, dk_acc, dv_acc,
):
    row_count = q_ref.shape[1]
    scale = HEAD_DIM ** (-0.5)
    dk_acc[...] = jnp.zeros_like(dk_acc)
    dv_acc[...] = jnp.zeros_like(dv_acc)
    for start in range(0, row_count, block_rows):
        finish = start + block_rows
        rows = slice(start, finish)
        queries = q_ref[:, rows].reshape(GROUP * block_rows, HEAD_DIM)
        grads = do_ref[:, rows].reshape(GROUP * block_rows, HEAD_DIM)
        scores = masked_scores(
            query_ids[rows], key_ids[:, :finish], queries, k_ref[0, :finish], start, finish, block_rows
        ).reshape(GROUP * block_rows, finish)
        probability = jnp.exp(scores - lse_ref[:, rows].reshape(GROUP * block_rows, 1))
        d_prob = lax.dot_general(
            grads, v_ref[0, :finish], (((1,), (1,)), ((), ())), preferred_element_type=jnp.float32
        )
        product = d_prob * probability
        d_scores = product - probability * jnp.sum(product, axis=-1, keepdims=True)
        d_scores = d_scores.astype(jnp.bfloat16)
        low_prob = probability.astype(jnp.bfloat16)
        dv_acc[:finish] += weight_grad(low_prob, grads)
        dk_acc[:finish] += weight_grad(d_scores, queries)
        d_query = jnp.dot(d_scores, k_ref[0, :finish], preferred_element_type=jnp.float32) * scale
        for head in range(GROUP):
            piece = d_query[head * block_rows : (head + 1) * block_rows]
            dq_ref[head, rows] = turn_back(piece, cos_ref[rows], sin_ref[rows]).astype(jnp.bfloat16)
    dk_ref[0] = turn_back(dk_acc[...] * scale, cos_ref[...], sin_ref[...]).astype(jnp.bfloat16)
    dv_ref[0] = dv_acc[...].astype(jnp.bfloat16)


def whole(shape):
    return pl.BlockSpec(shape, lambda j: (0,) * len(shape))


def per_kv(shape):
    return pl.BlockSpec(shape, lambda j: (j,) + (0,) * (len(shape) - 1))


def attend(query_rot, key_rot, values, ids, block_rows):
    row_count = query_rot.shape[1]
    group_spec = per_kv((GROUP, row_count, HEAD_DIM))
    one_spec = per_kv((1, row_count, HEAD_DIM))
    return pl.pallas_call(
        functools.partial(attend_kernel, block_rows),
        grid=(KV_HEADS,),
        out_shape=(
            jax.ShapeDtypeStruct((HEADS, row_count, HEAD_DIM), jnp.bfloat16),
            jax.ShapeDtypeStruct((HEADS, row_count, 1), jnp.float32),
        ),
        in_specs=[whole((row_count, 1)), whole((1, row_count)), group_spec, one_spec, one_spec],
        out_specs=(group_spec, per_kv((GROUP, row_count, 1))),
        compiler_params=pltpu.CompilerParams(vmem_limit_bytes=VMEM_LIMIT),
    )(ids[:, None], ids[None, :], query_rot, key_rot, values)


def attend_back(query_rot, key_rot, values, d_heads, log_total, cos_table, sin_table, ids, block_rows):
    row_count = query_rot.shape[1]
    group_spec = per_kv((GROUP, row_count, HEAD_DIM))
    one_spec = per_kv((1, row_count, HEAD_DIM))
    table_spec = whole((row_count, HEAD_DIM))
    return pl.pallas_call(
        functools.partial(attend_back_kernel, block_rows),
        grid=(KV_HEADS,),
        out_shape=(
            jax.ShapeDtypeStruct((HEADS, row_count, HEAD_DIM), jnp.bfloat16),
            jax.ShapeDtypeStruct((KV_HEADS, row_count, HEAD_DIM), jnp.bfloat16),
            jax.ShapeDtypeStruct((KV_HEADS, row_count, HEAD_DIM), jnp.bfloat16),
        ),
        in_specs=[
            whole((row_count, 1)), whole((1, row_count)), table_spec, table_spec,
            group_spec, one_spec, one_spec, group_spec, per_kv((GROUP, row_count, 1)),
        ],
        out_specs=(group_spec, one_spec, one_spec),
        scratch_shapes=[
            pltpu.VMEM((row_count, HEAD_DIM), jnp.float32),
            pltpu.VMEM((row_count, HEAD_DIM), jnp.float32),
        ],
        compiler_params=pltpu.CompilerParams(vmem_limit_bytes=VMEM_LIMIT),
    )(
        ids[:, None], ids[None, :], cos_table, sin_table,
        query_rot, key_rot, values, d_heads, log_total,
    )


def swiglu(gate_in, up_in):
    return jax.nn.silu(gate_in) * up_in


def packet_rows(lengths):
    return -(-sum(lengths) // (16 * LANES)) * 16


def gather_all(shards, device_count, collective_id):
    lengths = [shard.shape[0] for shard in shards]
    rows = packet_rows(lengths)
    pad = jnp.zeros((rows * LANES - sum(lengths),), shards[0].dtype)
    packet = jnp.concatenate(list(shards) + [pad]).reshape(rows, LANES)
    gathered = gather_packets(packet, device_count, collective_id)
    gathered = gathered.reshape(device_count, rows * LANES)
    pieces, at = [], 0
    for length in lengths:
        pieces.append(gathered[:, at : at + length].reshape(-1))
        at += length
    return pieces


def scatter_all(grads, device_count, collective_id):
    bit_count = device_count.bit_length() - 1
    lengths = [grad.size // device_count for grad in grads]
    rows = packet_rows(lengths)
    pad = jnp.zeros((device_count, rows * LANES - sum(lengths)), jnp.bfloat16)
    packets = jnp.concatenate(
        [grad.astype(jnp.bfloat16).reshape(device_count, -1) for grad in grads] + [pad], axis=1
    ).reshape((2,) * bit_count + (rows, LANES))
    summed = scatter_sums(packets, collective_id).reshape(-1)
    pieces, at = [], 0
    for length in lengths:
        pieces.append(summed[at : at + length])
        at += length
    return pieces


def split_heads(rows_in, head_count):
    return rows_in.reshape(rows_in.shape[0], head_count, HEAD_DIM).transpose(1, 0, 2)


def join_heads(heads_in):
    return heads_in.transpose(1, 0, 2).reshape(heads_in.shape[1], -1)


def turned_columns(weight):
    heads = weight.reshape(weight.shape[0], -1, 2, HEAD_DIM // 2)
    return jnp.stack([-heads[:, :, 1], heads[:, :, 0]], axis=2).reshape(weight.shape)


def local(
    tokens,
    segment_ids,
    cotangent,
    w_query,
    w_key,
    w_value,
    w_output,
    norm_gains,
    w_gate,
    w_up,
    w_down,
):
    row_count = tokens.shape[0]
    block_rows = min(256, row_count)
    kv_width = KV_HEADS * HEAD_DIM
    device_count = lax.axis_size("dp")
    full = gather_all(
        (w_query, w_key, w_value, w_output, w_gate, w_up, w_down, norm_gains), device_count, 0
    )
    weight_query = full[0].reshape(D, D)
    weight_key = full[1].reshape(D, kv_width)
    weight_value = full[2].reshape(D, kv_width)
    weight_output = full[3].reshape(D, D)
    weight_gate = full[4].reshape(D, FF)
    weight_up = full[5].reshape(D, FF)
    weight_down = full[6].reshape(FF, D)
    gain_one = full[7][:D].astype(jnp.float32)
    gain_two = full[7][D : 2 * D].astype(jnp.float32)

    position = jnp.arange(row_count, dtype=jnp.int32)
    ids = jnp.where(segment_ids >= 0, segment_ids, -1 - position)
    stream = tokens.astype(jnp.float32)
    cos_table, sin_table = rope_tables(segment_ids)
    attn_input = rms_norm(stream, gain_one).astype(jnp.bfloat16)
    weight_qk = jnp.concatenate([weight_query, weight_key], axis=1)
    straight = jnp.dot(attn_input, weight_qk, preferred_element_type=jnp.float32)
    turned = jnp.dot(attn_input, turned_columns(weight_qk), preferred_element_type=jnp.float32)
    repeat = HEADS + KV_HEADS
    rotated = straight * jnp.tile(cos_table, (1, repeat)) + turned * jnp.tile(sin_table, (1, repeat))
    rotated = split_heads(rotated.astype(jnp.bfloat16), repeat)
    query_rot, key_rot = (rotated[:HEADS], rotated[HEADS:])
    values = split_heads(
        jnp.dot(attn_input, weight_value, preferred_element_type=jnp.float32).astype(jnp.bfloat16),
        KV_HEADS,
    )
    mixture, log_total = attend(query_rot, key_rot, values, ids, block_rows)
    mixture = join_heads(mixture)
    stream_mid = stream + jnp.dot(mixture, weight_output, preferred_element_type=jnp.float32)
    mlp_input = rms_norm(stream_mid, gain_two).astype(jnp.bfloat16)
    gate = jnp.dot(mlp_input, weight_gate, preferred_element_type=jnp.float32)
    up_proj = jnp.dot(mlp_input, weight_up, preferred_element_type=jnp.float32)
    activation = swiglu(gate, up_proj).astype(jnp.bfloat16)
    layer_out = (
        stream_mid + jnp.dot(activation, weight_down, preferred_element_type=jnp.float32)
    ).astype(jnp.bfloat16)
    grad_down = weight_grad(activation, cotangent)
    d_act = input_grad(cotangent, weight_down)
    swiglu_out, swiglu_pull = jax.vjp(swiglu, gate, up_proj)
    d_gate, d_up = swiglu_pull(d_act)
    d_gate = d_gate.astype(jnp.bfloat16)
    d_up = d_up.astype(jnp.bfloat16)
    grad_gate = weight_grad(mlp_input, d_gate)
    grad_up = weight_grad(mlp_input, d_up)
    d_mlp_input = input_grad(d_gate, weight_gate) + input_grad(d_up, weight_up)
    norm_two_out, norm_two_pull = jax.vjp(rms_norm, stream_mid, gain_two)
    d_mid_norm, d_gain_two = norm_two_pull(d_mlp_input)
    d_mid = cotangent.astype(jnp.float32) + d_mid_norm
    d_attn = d_mid.astype(jnp.bfloat16)
    grad_output = weight_grad(mixture, d_attn)
    d_heads = split_heads(input_grad(d_attn, weight_output).astype(jnp.bfloat16), HEADS)
    d_query, d_key, d_value = attend_back(
        query_rot, key_rot, values, d_heads, log_total, cos_table, sin_table, ids, block_rows
    )
    d_query, d_key, d_value = (join_heads(d_query), join_heads(d_key), join_heads(d_value))
    grad_query = weight_grad(attn_input, d_query)
    grad_key = weight_grad(attn_input, d_key)
    grad_value = weight_grad(attn_input, d_value)
    d_attn_input = (
        input_grad(d_query, weight_query)
        + input_grad(d_key, weight_key)
        + input_grad(d_value, weight_value)
    )
    norm_one_out, norm_one_pull = jax.vjp(rms_norm, stream, gain_one)
    d_stream_norm, d_gain_one = norm_one_pull(d_attn_input)
    tokens_grad = (d_mid + d_stream_norm).astype(jnp.bfloat16)
    gain_total = norm_gains.shape[0] * device_count
    grad_gain_all = jnp.concatenate(
        [d_gain_one, d_gain_two, jnp.zeros((gain_total - 2 * D,), jnp.float32)]
    )
    parts = scatter_all(
        (
            grad_query, grad_key, grad_value, grad_output,
            grad_gate, grad_up, grad_down, grad_gain_all,
        ),
        device_count,
        1,
    )
    return (
        layer_out,
        tokens_grad,
        parts[0],
        parts[1],
        parts[2],
        parts[3],
        parts[7],
        parts[4],
        parts[5],
        parts[6],
    )


def solution(mesh):
    return jax.shard_map(
        local,
        mesh=mesh,
        in_specs=(
            P("dp", None),
            P("dp"),
            P("dp", None),
            P("dp"),
            P("dp"),
            P("dp"),
            P("dp"),
            P("dp"),
            P("dp"),
            P("dp"),
            P("dp"),
        ),
        out_specs=(
            P("dp", None),
            P("dp", None),
            P("dp"),
            P("dp"),
            P("dp"),
            P("dp"),
            P("dp"),
            P("dp"),
            P("dp"),
            P("dp"),
        ),
        check_vma=False,
    )
```
